128 devices in a mesh: ctx: 8 (over y, x_hi), tp: 16 (over x_lo, z, core).
Axes of the slice: x: 4 (x_hi: 2, x_lo: 2; x = x_hi * 2 + x_lo), y: 4, z: 4, core: 2. Of those that a mesh axis runs over, the one named last changes fastest.
Arguments:
- hidden: bfloat16 [2048, 53248], P('ctx', 'tp'), may hold values from -6 to 6
- sign_bits: int32 [53248], P('tp'), may hold values from 0 to 1
- weight_codes: int32 [53248, 8192], P('tp', 'ctx'), may hold values from 0 to 15
- weight_exps: int32 [1664, 8192], P('tp', 'ctx'), may hold values from 0 to 3
Outputs:
- projected: float32 [2048, 8192], P('tp', 'ctx')
The draws below stay inside these ranges and needn't reach their ends.
All inputs are finite; a program needn't handle non-finite values.
Results may differ from the reference program's by a relative error of at most 0.0029.
Values may be sent and summed in bfloat16 or wider, within the bound.
No kernel may reach another device: no remote copies, remote signals or barrier semaphores. Data moves between devices by JAX's collectives and lax.ppermute only.
A program may use at most 256 MiB of HBM per device.

```python
import math
import jax
import jax.numpy as jnp
import numpy as np
from jax import lax

D = 8192
PAL = 52
SYLV = 1024
FF = 53248
TOKENS = 2048
N_CTX = 8


def with_ends(drawn, stream_key, least, largest):
    place = [jax.random.randint(jax.random.fold_in(stream_key, axis), (), 0, length) for axis, length in enumerate(drawn.shape)]
    main_axis = drawn.shape.index(max(drawn.shape))
    neighbour = place[:main_axis] + [(place[main_axis] + 1) % drawn.shape[main_axis]] + place[main_axis + 1:]
    return drawn.at[tuple(place)].set(least).at[tuple(neighbour)].set(largest)


def block_scale(key, shape, split, smallest, high):
    def one(dim, shards_of):
        draws = jax.random.uniform(jax.random.fold_in(jax.random.fold_in(key, 6), dim), (shards_of,), jnp.float32, smallest / len(split), high / len(split))
        return jnp.repeat(jnp.exp(draws), shape[dim] // shards_of).reshape((-1,) + (1,) * (len(shape) - dim - 1))

    factor_of = one(*split[0])
    for cut in split[1:]:
        factor_of = factor_of * one(*cut)
    return factor_of


def centred(own_key, extent, width, reach, split=(), dtype=jnp.bfloat16):
    drawn = jax.random.normal(own_key, extent, jnp.float32) * width
    if len(split) > 0:
        drawn = block_scale(own_key, extent, split, -0.22, 0.18) * drawn
    return jnp.clip(drawn, min=-reach, max=reach).astype(dtype)


def setup_inputs(seed: int = 0) -> dict:
    key_of = jax.random.split(jax.random.key(seed), 5)
    hidden = centred(key_of[0], (TOKENS, FF), 1.0, 6.0, ((0, 8), (1, 16)))
    sign_bits = with_ends(jax.random.randint(key_of[1], (FF,), 0, 2), jax.random.fold_in(key_of[1], 1), 0, 1).astype(jnp.int32)
    weight_codes = with_ends(jax.random.randint(key_of[2], (FF, D), 0, 16), jax.random.fold_in(key_of[2], 1), 0, 15).astype(jnp.int32)
    weight_exps = with_ends(jax.random.randint(key_of[3], (FF // 32, D), 0, 4), jax.random.fold_in(key_of[3], 1), 0, 3).astype(jnp.int32)
    return {"hidden": hidden, "sign_bits": sign_bits, "weight_codes": weight_codes, "weight_exps": weight_exps}


def paley_matrix():
    elements = [(first_part, second_part) for first_part in range(5) for second_part in range(5)]
    squares = set()
    for left_elem in elements:
        if left_elem != (0, 0):
            squares.add(((left_elem[0] * left_elem[0] + 3 * left_elem[1] * left_elem[1]) % 5, 2 * left_elem[0] * left_elem[1] % 5))
    jacobs = np.zeros((25, 25))
    for row_index in range(25):
        for col_index in range(25):
            left_elem = elements[row_index]
            right_elem = elements[col_index]
            differ = ((left_elem[0] - right_elem[0]) % 5, (left_elem[1] - right_elem[1]) % 5)
            if differ == (0, 0):
                jacobs[row_index, col_index] = 0.0
            elif differ in squares:
                jacobs[row_index, col_index] = 1.0
            else:
                jacobs[row_index, col_index] = -1.0
    conference = np.zeros((26, 26))
    conference[0, 1:] = 1.0
    conference[1:, 0] = 1.0
    conference[1:, 1:] = jacobs
    result = np.kron(conference, np.array([[1.0, 1.0], [1.0, -1.0]])) + np.kron(np.eye(26), np.array([[1.0, -1.0], [-1.0, -1.0]]))
    return result

def sylvester(matrix_order):
    row_ids = lax.broadcasted_iota(jnp.int32, (matrix_order, matrix_order), 0)
    col_ids = lax.broadcasted_iota(jnp.int32, (matrix_order, matrix_order), 1)
    shared = jnp.bitwise_and(row_ids, col_ids)
    parity = jnp.zeros((matrix_order, matrix_order), jnp.int32)
    for bit_index in range(matrix_order.bit_length() - 1):
        parity = jnp.bitwise_xor(parity, jnp.bitwise_and(jnp.right_shift(shared, bit_index), 1))
    return (1 - 2 * parity).astype(jnp.float32)

def decode_weights(codes, exponents):
    magnitude = jnp.bitwise_and(codes, 7).astype(jnp.float32)
    value = jnp.where(magnitude < 4.0, magnitude * 0.5, jnp.where(magnitude < 6.0, magnitude - 2.0, 2.0 * magnitude - 8.0))
    value = jnp.where(codes >= 8, -value, value)
    scales = jnp.where(exponents == 0, 2.0 ** (-11), jnp.where(exponents == 1, 2.0 ** (-10), jnp.where(exponents == 2, 2.0 ** (-9), 2.0 ** (-8)))).astype(jnp.float32)
    blocks = value.reshape(codes.shape[0] // 32, 32, codes.shape[1]) * scales[:, None, :]
    return blocks.reshape(codes.shape).astype(jnp.bfloat16)

def reference(hidden, sign_bits, weight_codes, weight_exps):
    tokens_all = hidden.shape[0]
    flips = (1 - 2 * sign_bits).astype(jnp.float32)
    signed = hidden.astype(jnp.float32) * flips[None, :]
    folded = signed.reshape(tokens_all, SYLV, PAL)
    paley = jnp.asarray(paley_matrix(), jnp.float32)
    folded = jnp.einsum('rbp,pq->rbq', folded, paley, precision=lax.Precision.HIGHEST)
    folded = jnp.einsum('rbq,bc->rcq', folded, sylvester(SYLV), precision=lax.Precision.HIGHEST)
    rotated = (folded.reshape(tokens_all, FF) * (1.0 / math.sqrt(FF))).astype(jnp.bfloat16)
    columns = D // N_CTX
    outputs = []
    for shard_index in range(N_CTX):
        codes = weight_codes[:, shard_index * columns:(shard_index + 1) * columns]
        exponents = weight_exps[:, shard_index * columns:(shard_index + 1) * columns]
        weight_down = decode_weights(codes, exponents)
        outputs.append(jnp.dot(rotated, weight_down, preferred_element_type=jnp.float32))
    return jnp.concatenate(outputs, axis=1)
```

```python
import math

import jax
import jax.numpy as jnp
import numpy as np
from jax import lax
from jax.experimental import pallas as pl
from jax.experimental.pallas import tpu as pltpu
from jax.sharding import PartitionSpec as P


def paley_matrix():
    elements = [(first_part, second_part) for first_part in range(5) for second_part in range(5)]
    squares = set()
    for left_elem in elements:
        if left_elem != (0, 0):
            squares.add(
                (
                    (left_elem[0] * left_elem[0] + 3 * left_elem[1] * left_elem[1]) % 5,
                    2 * left_elem[0] * left_elem[1] % 5,
                )
            )
    jacobs = np.zeros((25, 25))
    for row_index in range(25):
        for col_index in range(25):
            left_elem = elements[row_index]
            right_elem = elements[col_index]
            differ = ((left_elem[0] - right_elem[0]) % 5, (left_elem[1] - right_elem[1]) % 5)
            if differ == (0, 0):
                jacobs[row_index, col_index] = 0.0
            elif differ in squares:
                jacobs[row_index, col_index] = 1.0
            else:
                jacobs[row_index, col_index] = -1.0
    conference = np.zeros((26, 26))
    conference[0, 1:] = 1.0
    conference[1:, 0] = 1.0
    conference[1:, 1:] = jacobs
    result = np.kron(conference, np.array([[1.0, 1.0], [1.0, -1.0]])) + np.kron(
        np.eye(26), np.array([[1.0, -1.0], [-1.0, -1.0]])
    )
    return result


def sylvester(order):
    matrix = np.ones((1, 1))
    while matrix.shape[0] < order:
        matrix = np.kron(np.array([[1.0, 1.0], [1.0, -1.0]]), matrix)
    return matrix


def decode_weights(codes, exponents):
    magnitude = jnp.bitwise_and(codes, 7).astype(jnp.float32)
    value = jnp.where(
        magnitude < 4.0,
        magnitude * 0.5,
        jnp.where(magnitude < 6.0, magnitude - 2.0, 2.0 * magnitude - 8.0),
    )
    value = jnp.where(codes >= 8, -value, value)
    scales = jnp.where(
        exponents == 0,
        2.0 ** (-11),
        jnp.where(
            exponents == 1, 2.0 ** (-10), jnp.where(exponents == 2, 2.0 ** (-9), 2.0 ** (-8))
        ),
    ).astype(jnp.float32)
    blocks = value.reshape(codes.shape[0] // 32, 32, codes.shape[1]) * scales[:, None, :]
    return blocks.reshape(codes.shape).astype(jnp.bfloat16)


def butterfly(total, distance):
    rows, width = total.shape
    if distance % 8 == 0:
        pairs = total.reshape(rows // (2 * distance), 2, distance, width)
        low, high = pairs[:, 0], pairs[:, 1]
        return jnp.stack([low + high, low - high], axis=1).reshape(rows, width)
    tiles = total.reshape(rows // 8, 8, width)
    other = pltpu.roll(tiles, 4, 1)
    place = lax.broadcasted_iota(jnp.int32, tiles.shape, 1)
    return jnp.where(place < 4, tiles + other, other - tiles).reshape(rows, width)


def rotate_kernel(share, scaling, rows_ref, matrix_ref, out_ref):
    half = matrix_ref.shape[0]
    for start in range(0, half, 256):
        width = min(256, half - start)
        columns = matrix_ref[:, start : start + width]
        low = jnp.dot(rows_ref[:, :half], columns, preferred_element_type=jnp.float32)
        high = jnp.dot(rows_ref[:, half:], columns, preferred_element_type=jnp.float32)
        for place, total in ((0, low + high), (half, low - high)):
            distance = share
            while distance < rows_ref.shape[0]:
                total = butterfly(total, distance)
                distance *= 2
            out_ref[:, place + start : place + start + width] = (total * scaling).astype(
                jnp.bfloat16
            )


def rotate(raw, matrix):
    groups, share, width = raw.shape
    scaling = 1.0 / math.sqrt(groups * width)
    rotated = pl.pallas_call(
        lambda *refs: rotate_kernel(share, scaling, *refs),
        out_shape=jax.ShapeDtypeStruct((groups * share, width), jnp.bfloat16),
        in_specs=[pl.BlockSpec(memory_space=pltpu.VMEM)] * 2,
        out_specs=pl.BlockSpec(memory_space=pltpu.VMEM),
        compiler_params=pltpu.CompilerParams(vmem_limit_bytes=40 * 1024 * 1024),
        cost_estimate=pl.CostEstimate(
            flops=2 * groups * share * width * (width // 2),
            bytes_accessed=width * width // 2 + 4 * groups * share * width,
            transcendentals=0,
        ),
    )(raw.reshape(groups * share, width), matrix)
    return rotated.reshape(groups, share, width)


CHUNKS = 1


def shards(hidden, sign_bits, weight_codes, weight_exps):
    tokens, width = hidden.shape
    groups = lax.axis_size("tp")
    n_ctx = lax.axis_size("ctx")
    owners_here = groups // n_ctx
    piece = tokens // owners_here // CHUNKS
    matrix = jnp.asarray(np.kron(sylvester(width // 104), paley_matrix()), jnp.bfloat16)
    signed = hidden * (1 - 2 * sign_bits).astype(jnp.bfloat16)[None, :]
    cut = signed.reshape(owners_here, CHUNKS, piece, width)
    weight_down = decode_weights(weight_codes, weight_exps)
    outs = []
    for chunk in range(CHUNKS):
        raw = cut[:, chunk].reshape(groups, owners_here * piece // groups, width)
        raw = lax.all_to_all(raw, "tp", 0, 0, tiled=True)
        rotated = rotate(raw, matrix)
        rotated = lax.all_to_all(rotated, "tp", 0, 0, tiled=True)
        rotated = rotated.reshape(owners_here * piece, width)
        gathered = lax.all_gather(rotated, "ctx", axis=0, tiled=True)
        partial = jnp.dot(gathered, weight_down, preferred_element_type=jnp.float32)
        outs.append(lax.psum_scatter(partial, "tp", scatter_dimension=0, tiled=True))
    return jnp.concatenate(outs, axis=0)


def solution(mesh):
    return jax.shard_map(
        shards,
        mesh=mesh,
        in_specs=(P("ctx", "tp"), P("tp"), P("tp", "ctx"), P("tp", "ctx")),
        out_specs=P("tp", "ctx"),
        check_vma=False,
    )
```

```python
import math

import jax
import jax.numpy as jnp
import numpy as np
from jax import lax
from jax.experimental import pallas as pl
from jax.experimental.pallas import tpu as pltpu
from jax.sharding import PartitionSpec as P


def paley_matrix():
    elements = [(first_part, second_part) for first_part in range(5) for second_part in range(5)]
    squares = set()
    for left_elem in elements:
        if left_elem != (0, 0):
            squares.add(
                (
                    (left_elem[0] * left_elem[0] + 3 * left_elem[1] * left_elem[1]) % 5,
                    2 * left_elem[0] * left_elem[1] % 5,
                )
            )
    jacobs = np.zeros((25, 25))
    for row_index in range(25):
        for col_index in range(25):
            left_elem = elements[row_index]
            right_elem = elements[col_index]
            differ = ((left_elem[0] - right_elem[0]) % 5, (left_elem[1] - right_elem[1]) % 5)
            if differ == (0, 0):
                jacobs[row_index, col_index] = 0.0
            elif differ in squares:
                jacobs[row_index, col_index] = 1.0
            else:
                jacobs[row_index, col_index] = -1.0
    conference = np.zeros((26, 26))
    conference[0, 1:] = 1.0
    conference[1:, 0] = 1.0
    conference[1:, 1:] = jacobs
    result = np.kron(conference, np.array([[1.0, 1.0], [1.0, -1.0]])) + np.kron(
        np.eye(26), np.array([[1.0, -1.0], [-1.0, -1.0]])
    )
    return result


def sylvester(order):
    matrix = np.ones((1, 1))
    while matrix.shape[0] < order:
        matrix = np.kron(np.array([[1.0, 1.0], [1.0, -1.0]]), matrix)
    return matrix


def decode_kernel(codes_ref, exps_ref, out_ref):
    for block in range(exps_ref.shape[0]):
        codes = codes_ref[block * 32 : block * 32 + 32, :]
        scale = jnp.left_shift(1, exps_ref[block : block + 1, :]).astype(jnp.float32) * 2.0 ** (-11)
        scale = jnp.where(codes >= 8, -scale, scale)
        magnitude = jnp.bitwise_and(codes, 7).astype(jnp.float32)
        value = jnp.where(
            magnitude < 4.0,
            magnitude * 0.5,
            jnp.where(magnitude < 6.0, magnitude - 2.0, 2.0 * magnitude - 8.0),
        )
        out_ref[block * 32 : block * 32 + 32, :] = (value * scale).astype(jnp.bfloat16)


def decode_weights(codes, exponents):
    rows, columns = codes.shape
    step = 256
    return pl.pallas_call(
        decode_kernel,
        grid=(rows // step,),
        out_shape=jax.ShapeDtypeStruct(codes.shape, jnp.bfloat16),
        in_specs=[
            pl.BlockSpec((step, columns), lambda i: (i, 0)),
            pl.BlockSpec((step // 32, columns), lambda i: (i, 0)),
        ],
        out_specs=pl.BlockSpec((step, columns), lambda i: (i, 0)),
        compiler_params=pltpu.CompilerParams(vmem_limit_bytes=56 * 1024 * 1024),
        cost_estimate=pl.CostEstimate(
            flops=10 * rows * columns, bytes_accessed=6 * rows * columns, transcendentals=0
        ),
    )(codes, exponents)


def butterfly(parts):
    distance = 1
    while distance < len(parts):
        parts = [
            parts[index] + parts[index + distance]
            if index // distance % 2 == 0
            else parts[index - distance] - parts[index]
            for index in range(len(parts))
        ]
        distance *= 2
    return parts


def rotate_kernel(share, scaling, rows_ref, matrix_ref, out_ref, total_ref, columns_ref, arrived):
    half = matrix_ref.shape[0]
    starts = list(range(0, half, 256))
    copies = []
    for index, start in enumerate(starts):
        window = pl.ds(start, min(256, half - start))
        copies.append(
            pltpu.make_async_copy(
                matrix_ref.at[:, window], columns_ref.at[:, window], arrived.at[index]
            )
        )
    for copy in copies:
        copy.start()
    stacked = jnp.concatenate([rows_ref[:, :half], rows_ref[:, half:]], axis=0)
    for index, start in enumerate(starts):
        width = min(256, half - start)
        copies[index].wait()
        columns = columns_ref[:, start : start + width]
        total_ref[:, :width] = jnp.dot(stacked, columns, preferred_element_type=jnp.float32)
        count = rows_ref.shape[0]
        for lane in range(0, width, 128):
            low, high = (
                [
                    total_ref[base + at : base + at + share, lane : lane + 128]
                    for at in range(0, count, share)
                ]
                for base in (0, count)
            )
            window = slice(start + lane, start + lane + 128)
            other = slice(half + start + lane, half + start + lane + 128)
            for at, (one, two) in enumerate(zip(butterfly(low), butterfly(high))):
                out_ref[at, :, window] = ((one + two) * scaling).astype(jnp.bfloat16)
                out_ref[at, :, other] = ((one - two) * scaling).astype(jnp.bfloat16)


def rotate(raw, matrix):
    groups, share, width = raw.shape
    scaling = 1.0 / math.sqrt(groups * width)
    return pl.pallas_call(
        lambda *refs: rotate_kernel(share, scaling, *refs),
        out_shape=jax.ShapeDtypeStruct(raw.shape, jnp.bfloat16),
        in_specs=[
            pl.BlockSpec(memory_space=pltpu.VMEM),
            pl.BlockSpec(memory_space=pl.ANY),
        ],
        out_specs=pl.BlockSpec(memory_space=pltpu.VMEM),
        scratch_shapes=[
            pltpu.VMEM((2 * groups * share, 256), jnp.float32),
            pltpu.VMEM(matrix.shape, jnp.bfloat16),
            pltpu.SemaphoreType.DMA((-(-matrix.shape[0] // 256),)),
        ],
        compiler_params=pltpu.CompilerParams(vmem_limit_bytes=56 * 1024 * 1024),
        cost_estimate=pl.CostEstimate(
            flops=2 * groups * share * width * (width // 2),
            bytes_accessed=width * width // 2 + 4 * groups * share * width,
            transcendentals=0,
        ),
    )(raw.reshape(groups * share, width), matrix)


def block_of(place_ref, shift):
    return lax.rem(place_ref[0] + shift[0], 4) * 2 + lax.rem(place_ref[1] + shift[1], 2)


def product_kernel(spec, shifts, place_ref, weight_ref, *refs):
    pieces = refs[:-3]
    out_ref, rows_ref, arrived = refs[-3:]
    blocks, n_rows, width = rows_ref.shape

    @pl.when(pl.program_id(0) == 0)
    def _():
        copies = []
        for index, (source, begin, count, block, start) in enumerate(spec):
            window = rows_ref.at[block, pl.ds(start, count)]
            block_rows = pieces[source].at[pl.ds(begin, count)]
            copies.append(pltpu.make_async_copy(block_rows, window, arrived.at[index]))
        for copy in copies:
            copy.start()
        for copy in copies:
            copy.wait()

    total = (
        jnp.dot(
            rows_ref[...].reshape(blocks * n_rows, width),
            weight_ref[...],
            preferred_element_type=jnp.float32,
        )
        .reshape(blocks, n_rows, weight_ref.shape[1])
        .astype(jnp.bfloat16)
    )
    for block, shift in enumerate(shifts):
        out_ref[block_of(place_ref, shift)] = total[block]


def product(place, weight, spec, pieces):
    width, columns = weight.shape
    tile = 256
    blocks = 7
    rows = sum(piece.shape[0] for piece in pieces) // blocks
    shifts = [(0, 0), (3, 0), (1, 0), (2, 0), (0, 1), (3, 1), (1, 1)]
    return pl.pallas_call(
        lambda *refs: product_kernel(spec, shifts, *refs),
        grid=(columns // tile,),
        out_shape=jax.ShapeDtypeStruct((blocks + 1, rows, columns), jnp.bfloat16),
        in_specs=[
            pl.BlockSpec(memory_space=pltpu.SMEM),
            pl.BlockSpec((width, tile), lambda i: (0, i)),
        ]
        + [pl.BlockSpec(memory_space=pl.ANY)] * len(pieces),
        out_specs=pl.BlockSpec((blocks + 1, rows, tile), lambda i: (0, 0, i)),
        scratch_shapes=[
            pltpu.VMEM((blocks, rows, width), jnp.bfloat16),
            pltpu.SemaphoreType.DMA((len(spec),)),
        ],
        compiler_params=pltpu.CompilerParams(vmem_limit_bytes=56 * 1024 * 1024),
        cost_estimate=pl.CostEstimate(
            flops=50 * blocks * rows * width * columns,
            bytes_accessed=2 * (width * columns + blocks * rows * (width + columns)),
            transcendentals=0,
        ),
    )(place, weight, *pieces)


def last_kernel(place_ref, weight_ref, before_ref, low_ref, high_ref, out_ref, rows_ref, total_ref, arrived):
    step = pl.program_id(0)
    half = low_ref.shape[0]
    tile = weight_ref.shape[1]

    @pl.when(step == 0)
    def _():
        rows_ref[:half] = low_ref[...]
        rows_ref[half:] = high_ref[...]

    total_ref[step] = jnp.dot(
        rows_ref[...], weight_ref[...], preferred_element_type=jnp.float32
    ).astype(jnp.bfloat16)

    @pl.when(step == total_ref.shape[0] - 1)
    def _():
        copies = []
        for index in range(total_ref.shape[0]):
            window = out_ref.at[block_of(place_ref, (2, 1)), :, pl.ds(index * tile, tile)]
            copies.append(pltpu.make_async_copy(total_ref.at[index], window, arrived.at[index]))
        for copy in copies:
            copy.start()
        for copy in copies:
            copy.wait()


def product_last(place, weight, before, low, high):
    width, columns = weight.shape
    tile = 256
    rows = 2 * low.shape[0]
    return pl.pallas_call(
        last_kernel,
        grid=(columns // tile,),
        out_shape=jax.ShapeDtypeStruct(before.shape, jnp.bfloat16),
        in_specs=[
            pl.BlockSpec(memory_space=pltpu.SMEM),
            pl.BlockSpec((width, tile), lambda i: (0, i)),
            pl.BlockSpec(memory_space=pl.ANY),
            pl.BlockSpec(low.shape, lambda i: (0, 0)),
            pl.BlockSpec(high.shape, lambda i: (0, 0)),
        ],
        out_specs=pl.BlockSpec(memory_space=pl.ANY),
        scratch_shapes=[
            pltpu.VMEM((rows, width), jnp.bfloat16),
            pltpu.VMEM((columns // tile, rows, tile), jnp.bfloat16),
            pltpu.SemaphoreType.DMA((columns // tile,)),
        ],
        input_output_aliases={2: 0},
        compiler_params=pltpu.CompilerParams(vmem_limit_bytes=56 * 1024 * 1024),
        cost_estimate=pl.CostEstimate(
            flops=2 * rows * width * columns,
            bytes_accessed=2 * (width * columns + rows * (width + columns)),
            transcendentals=0,
        ),
    )(place, weight, before, low, high)


def ring(step):
    def move(block):
        count = lax.axis_size("ctx")
        return lax.ppermute(block, "ctx", [(i, (i + 2 * step) % count) for i in range(count)])

    return move


def across(block):
    return lax.ppermute(block, "ctx", [(i, i ^ 1) for i in range(lax.axis_size("ctx"))])


def exchange(block):
    return lax.all_to_all(block, "tp", 0, 0, tiled=True)


def sync(*values):
    return lax.optimization_barrier(values)


def keep(*values):
    return values

def shards(hidden, sign_bits, weight_codes, weight_exps):
    tokens, width = hidden.shape
    columns = weight_codes.shape[1]
    groups = lax.axis_size("tp")
    share = tokens // groups // 2
    matrix = jnp.asarray(np.kron(sylvester(width // 104), paley_matrix()), jnp.bfloat16)
    flips = (1 - 2 * sign_bits).astype(jnp.bfloat16)
    ctx = lax.axis_index("ctx")
    place = jnp.stack([ctx // 2, ctx % 2]).astype(jnp.int32)
    up, down = ring(1), ring(-1)
    rows = tokens // 2
    half, quarter = rows // 2, rows // 4
    got = exchange((hidden * flips).reshape(groups, 2 * share, width))
    weight = decode_weights(weight_codes, weight_exps)
    got, weight = sync(got, weight)
    own0 = exchange(rotate(got[:, :share], matrix)).reshape(rows, width)
    rotated1 = rotate(got[:, share:], matrix)
    own0, rotated1, weight = keep(own0, rotated1, weight)

    below0, above0, other0 = up(own0), down(own0), across(own0)
    own1 = exchange(rotated1).reshape(rows, width)
    below0, above0, other0, own1, weight = keep(below0, above0, other0, own1, weight)

    other_below0, other_above0 = up(other0[:half]), down(other0[:half])
    far0 = [up(below0[:half]), down(above0[half:])]
    late0 = across(jnp.concatenate([below0[half:], above0[half:]]))
    other_below0, other_above0, late0, own1, *far0 = keep(
        other_below0, other_above0, late0, own1, *far0
    )

    spec = [
        (0, 0, rows, 0, 0),
        (1, 0, rows, 1, 0),
        (2, 0, rows, 2, 0),
        (3, 0, half, 3, 0),
        (4, 0, half, 3, half),
        (5, 0, rows, 4, 0),
        (6, 0, half, 5, 0),
        (7, 0, half, 6, 0),
        (8, 0, half, 5, half),
        (8, half, half, 6, half),
    ]
    last0 = up(other_below0)
    late_far0 = across(far0[1])
    below1, above1, other1 = up(own1), down(own1), across(own1)
    pieces0 = [own0, below0, above0, *far0, other0, other_below0, other_above0, late0]
    part0 = product(place, weight, spec, pieces0)
    below1, above1, other1, late_far0, part0, last0 = keep(
        below1, above1, other1, late_far0, part0, last0
    )

    part0 = product_last(place, weight, part0, last0, late_far0)
    sent0 = exchange(part0.reshape(groups, half, columns))
    other_below1, other_above1 = up(other1), down(other1)
    far1 = [up(below1[:half]), down(above1[half:])]
    other_below1, other_above1, *far1 = keep(other_below1, other_above1, *far1)

    last1 = [up(other_below1[:half]), down(other_above1[half:])]
    spec1 = [(0, 0, rows, 0, 0), (1, 0, rows, 1, 0), (2, 0, rows, 2, 0), (3, 0, half, 3, 0)]
    spec1 += [(4, 0, half, 3, half), (5, 0, rows, 4, 0), (6, 0, rows, 5, 0), (7, 0, rows, 6, 0)]
    pieces1 = [own1, below1, above1, *far1, other1, other_below1, other_above1]
    part1 = product(place, weight, spec1, pieces1)
    part1, *last1 = keep(part1, *last1)
    part1 = product_last(place, weight, part1, *last1)
    sent1 = exchange(part1.reshape(groups, half, columns))
    outs = [
        jnp.sum(sent.astype(jnp.float32), axis=0).reshape(groups // 2, share, columns)
        for sent in (sent0, sent1)
    ]
    return jnp.concatenate(outs, axis=1).reshape(rows, columns)


def solution(mesh):
    return jax.shard_map(
        shards,
        mesh=mesh,
        in_specs=(P("ctx", "tp"), P("tp"), P("tp", "ctx"), P("tp", "ctx")),
        out_specs=P("tp", "ctx"),
        check_vma=False,
    )
```

```python
import math

import jax
import jax.numpy as jnp
import numpy as np
from jax import lax
from jax.experimental import pallas as pl
from jax.experimental.pallas import tpu as pltpu
from jax.sharding import PartitionSpec as P


def paley_matrix():
    elements = [(first_part, second_part) for first_part in range(5) for second_part in range(5)]
    squares = set()
    for left_elem in elements:
        if left_elem != (0, 0):
            squares.add(
                (
                    (left_elem[0] * left_elem[0] + 3 * left_elem[1] * left_elem[1]) % 5,
                    2 * left_elem[0] * left_elem[1] % 5,
                )
            )
    jacobs = np.zeros((25, 25))
    for row_index in range(25):
        for col_index in range(25):
            left_elem = elements[row_index]
            right_elem = elements[col_index]
            differ = ((left_elem[0] - right_elem[0]) % 5, (left_elem[1] - right_elem[1]) % 5)
            if differ == (0, 0):
                jacobs[row_index, col_index] = 0.0
            elif differ in squares:
                jacobs[row_index, col_index] = 1.0
            else:
                jacobs[row_index, col_index] = -1.0
    conference = np.zeros((26, 26))
    conference[0, 1:] = 1.0
    conference[1:, 0] = 1.0
    conference[1:, 1:] = jacobs
    result = np.kron(conference, np.array([[1.0, 1.0], [1.0, -1.0]])) + np.kron(
        np.eye(26), np.array([[1.0, -1.0], [-1.0, -1.0]])
    )
    return result


def sylvester(order):
    matrix = np.ones((1, 1))
    while matrix.shape[0] < order:
        matrix = np.kron(np.array([[1.0, 1.0], [1.0, -1.0]]), matrix)
    return matrix


def decode_kernel(codes_ref, exps_ref, out_ref):
    for block in range(exps_ref.shape[0]):
        codes = codes_ref[block * 32 : block * 32 + 32, :]
        scale = jnp.left_shift(1, exps_ref[block : block + 1, :]).astype(jnp.float32) * 2.0 ** (-11)
        scale = jnp.where(codes >= 8, -scale, scale)
        magnitude = jnp.bitwise_and(codes, 7).astype(jnp.float32)
        value = jnp.where(
            magnitude < 4.0,
            magnitude * 0.5,
            jnp.where(magnitude < 6.0, magnitude - 2.0, 2.0 * magnitude - 8.0),
        )
        out_ref[block * 32 : block * 32 + 32, :] = (value * scale).astype(jnp.bfloat16)


def decode_weights(codes, exponents):
    rows, columns = codes.shape
    step = 256
    return pl.pallas_call(
        decode_kernel,
        grid=(rows // step,),
        out_shape=jax.ShapeDtypeStruct(codes.shape, jnp.bfloat16),
        in_specs=[
            pl.BlockSpec((step, columns), lambda i: (i, 0)),
            pl.BlockSpec((step // 32, columns), lambda i: (i, 0)),
        ],
        out_specs=pl.BlockSpec((step, columns), lambda i: (i, 0)),
        compiler_params=pltpu.CompilerParams(vmem_limit_bytes=56 * 1024 * 1024),
        cost_estimate=pl.CostEstimate(
            flops=10 * rows * columns, bytes_accessed=6 * rows * columns, transcendentals=0
        ),
    )(codes, exponents)


def butterfly(parts):
    distance = 1
    while distance < len(parts):
        parts = [
            parts[index] + parts[index + distance]
            if index // distance % 2 == 0
            else parts[index - distance] - parts[index]
            for index in range(len(parts))
        ]
        distance *= 2
    return parts


def rotate_kernel(share, begin, scaling, raw_ref, matrix_ref, out_ref, total_ref, columns_ref, arrived):
    half = matrix_ref.shape[0]
    starts = list(range(0, half, 512))
    copies = []
    for index, start in enumerate(starts):
        window = pl.ds(start, min(512, half - start))
        copies.append(
            pltpu.make_async_copy(
                matrix_ref.at[:, window], columns_ref.at[:, window], arrived.at[index]
            )
        )
    for copy in copies:
        copy.start()
    rows = raw_ref[:, begin : begin + share, :].reshape(-1, 2 * half)
    stacked = jnp.concatenate([rows[:, :half], rows[:, half:]], axis=0)
    for index, start in enumerate(starts):
        width = min(512, half - start)
        copies[index].wait()
        columns = columns_ref[:, start : start + width]
        total_ref[:, :width] = jnp.dot(stacked, columns, preferred_element_type=jnp.float32)
        count = rows.shape[0]
        for lane in range(0, width, 128):
            low, high = (
                [
                    total_ref[base + at : base + at + share, lane : lane + 128]
                    for at in range(0, count, share)
                ]
                for base in (0, count)
            )
            window = slice(start + lane, start + lane + 128)
            other = slice(half + start + lane, half + start + lane + 128)
            for at, (one, two) in enumerate(zip(butterfly(low), butterfly(high))):
                out_ref[at, :, window] = ((one + two) * scaling).astype(jnp.bfloat16)
                out_ref[at, :, other] = ((one - two) * scaling).astype(jnp.bfloat16)


def rotate(raw, matrix, begin, share):
    groups, _, width = raw.shape
    scaling = 1.0 / math.sqrt(groups * width)
    return pl.pallas_call(
        lambda *refs: rotate_kernel(share, begin, scaling, *refs),
        out_shape=jax.ShapeDtypeStruct((groups, share, width), jnp.bfloat16),
        in_specs=[
            pl.BlockSpec(memory_space=pltpu.VMEM),
            pl.BlockSpec(memory_space=pl.ANY),
        ],
        out_specs=pl.BlockSpec(memory_space=pltpu.VMEM),
        scratch_shapes=[
            pltpu.VMEM((2 * groups * share, 512), jnp.float32),
            pltpu.VMEM(matrix.shape, jnp.bfloat16),
            pltpu.SemaphoreType.DMA((-(-matrix.shape[0] // 512),)),
        ],
        compiler_params=pltpu.CompilerParams(vmem_limit_bytes=56 * 1024 * 1024),
        cost_estimate=pl.CostEstimate(
            flops=2 * groups * share * width * (width // 2),
            bytes_accessed=width * width // 2 + 4 * groups * share * width,
            transcendentals=0,
        ),
    )(raw, matrix)


def block_of(place_ref, shift):
    return lax.rem(place_ref[0] + shift[0], 4) * 2 + lax.rem(place_ref[1] + shift[1], 2)


def product_kernel(spec, shifts, place_ref, weight_ref, *refs):
    pieces = refs[:-3]
    out_ref, rows_ref, arrived = refs[-3:]
    blocks, n_rows, width = rows_ref.shape

    @pl.when(pl.program_id(0) == 0)
    def _():
        copies = []
        for index, (source, begin, count, block, start) in enumerate(spec):
            window = rows_ref.at[block, pl.ds(start, count)]
            block_rows = pieces[source].at[pl.ds(begin, count)]
            copies.append(pltpu.make_async_copy(block_rows, window, arrived.at[index]))
        for copy in copies:
            copy.start()
        for copy in copies:
            copy.wait()

    total = (
        jnp.dot(
            rows_ref[...].reshape(blocks * n_rows, width),
            weight_ref[...],
            preferred_element_type=jnp.float32,
        )
        .reshape(blocks, n_rows, weight_ref.shape[1])
        .astype(jnp.bfloat16)
    )
    for block, shift in enumerate(shifts):
        out_ref[block_of(place_ref, shift)] = total[block]


def product(place, weight, spec, pieces):
    width, columns = weight.shape
    tile = 256
    blocks = 7
    rows = sum(piece.shape[0] for piece in pieces) // blocks
    shifts = [(0, 0), (3, 0), (1, 0), (2, 0), (0, 1), (3, 1), (1, 1)]
    return pl.pallas_call(
        lambda *refs: product_kernel(spec, shifts, *refs),
        grid=(columns // tile,),
        out_shape=jax.ShapeDtypeStruct((blocks + 1, rows, columns), jnp.bfloat16),
        in_specs=[
            pl.BlockSpec(memory_space=pltpu.SMEM),
            pl.BlockSpec((width, tile), lambda i: (0, i)),
        ]
        + [pl.BlockSpec(memory_space=pl.ANY)] * len(pieces),
        out_specs=pl.BlockSpec((blocks + 1, rows, tile), lambda i: (0, 0, i)),
        scratch_shapes=[
            pltpu.VMEM((blocks, rows, width), jnp.bfloat16),
            pltpu.SemaphoreType.DMA((len(spec),)),
        ],
        compiler_params=pltpu.CompilerParams(vmem_limit_bytes=56 * 1024 * 1024),
        cost_estimate=pl.CostEstimate(
            flops=50 * blocks * rows * width * columns,
            bytes_accessed=2 * (width * columns + blocks * rows * (width + columns)),
            transcendentals=0,
        ),
    )(place, weight, *pieces)


def last_kernel(place_ref, weight_ref, before_ref, low_ref, high_ref, out_ref, rows_ref, total_ref, arrived):
    step = pl.program_id(0)
    half = low_ref.shape[0]
    tile = weight_ref.shape[1]

    @pl.when(step == 0)
    def _():
        rows_ref[:half] = low_ref[...]
        rows_ref[half:] = high_ref[...]

    total_ref[step] = jnp.dot(
        rows_ref[...], weight_ref[...], preferred_element_type=jnp.float32
    ).astype(jnp.bfloat16)

    @pl.when(step == total_ref.shape[0] - 1)
    def _():
        copies = []
        for index in range(total_ref.shape[0]):
            window = out_ref.at[block_of(place_ref, (2, 1)), :, pl.ds(index * tile, tile)]
            copies.append(pltpu.make_async_copy(total_ref.at[index], window, arrived.at[index]))
        for copy in copies:
            copy.start()
        for copy in copies:
            copy.wait()


def product_last(place, weight, before, low, high):
    width, columns = weight.shape
    tile = 512
    rows = 2 * low.shape[0]
    return pl.pallas_call(
        last_kernel,
        grid=(columns // tile,),
        out_shape=jax.ShapeDtypeStruct(before.shape, jnp.bfloat16),
        in_specs=[
            pl.BlockSpec(memory_space=pltpu.SMEM),
            pl.BlockSpec((width, tile), lambda i: (0, i)),
            pl.BlockSpec(memory_space=pl.ANY),
            pl.BlockSpec(low.shape, lambda i: (0, 0)),
            pl.BlockSpec(high.shape, lambda i: (0, 0)),
        ],
        out_specs=pl.BlockSpec(memory_space=pl.ANY),
        scratch_shapes=[
            pltpu.VMEM((rows, width), jnp.bfloat16),
            pltpu.VMEM((columns // tile, rows, tile), jnp.bfloat16),
            pltpu.SemaphoreType.DMA((columns // tile,)),
        ],
        input_output_aliases={2: 0},
        compiler_params=pltpu.CompilerParams(vmem_limit_bytes=56 * 1024 * 1024),
        cost_estimate=pl.CostEstimate(
            flops=2 * rows * width * columns,
            bytes_accessed=2 * (width * columns + rows * (width + columns)),
            transcendentals=0,
        ),
    )(place, weight, before, low, high)


def split_product_kernel(spec, shifts, place_ref, weight_ref, *refs):
    pieces = refs[:-4]
    keep_ref, send_ref, rows_ref, arrived = refs[-4:]
    blocks, n_rows, width = rows_ref.shape

    @pl.when(pl.program_id(0) == 0)
    def _():
        copies = []
        for index, (source, begin, count, block, start) in enumerate(spec):
            window = rows_ref.at[block, pl.ds(start, count)]
            block_rows = pieces[source].at[pl.ds(begin, count)]
            copies.append(pltpu.make_async_copy(block_rows, window, arrived.at[index]))
        for copy in copies:
            copy.start()
        for copy in copies:
            copy.wait()

    total = jnp.dot(
        rows_ref[...].reshape(blocks * n_rows, width),
        weight_ref[...],
        preferred_element_type=jnp.float32,
    ).reshape(blocks, 2, n_rows // 2, weight_ref.shape[1])
    second = place_ref[2] == 1
    for block, shift in enumerate(shifts):
        where = block_of(place_ref, shift)
        low, high = total[block, 0], total[block, 1]
        keep_ref[where] = jnp.where(second, high, low)
        send_ref[where] = jnp.where(second, low, high).astype(jnp.bfloat16)


def split_product(place, weight, spec, pieces):
    width, columns = weight.shape
    tile = 256
    blocks = 7
    rows = sum(count for _, _, count, _, _ in spec) // blocks
    shifts = [(0, 0), (3, 0), (1, 0), (2, 0), (0, 1), (3, 1), (1, 1)]
    shape = (blocks + 1, rows // 2, columns)
    block = pl.BlockSpec((blocks + 1, rows // 2, tile), lambda i: (0, 0, i))
    return pl.pallas_call(
        lambda *refs: split_product_kernel(spec, shifts, *refs),
        grid=(columns // tile,),
        out_shape=[
            jax.ShapeDtypeStruct(shape, jnp.float32),
            jax.ShapeDtypeStruct(shape, jnp.bfloat16),
        ],
        in_specs=[
            pl.BlockSpec(memory_space=pltpu.SMEM),
            pl.BlockSpec((width, tile), lambda i: (0, i)),
        ]
        + [pl.BlockSpec(memory_space=pl.ANY)] * len(pieces),
        out_specs=[block, block],
        scratch_shapes=[
            pltpu.VMEM((blocks, rows, width), jnp.bfloat16),
            pltpu.SemaphoreType.DMA((len(spec),)),
        ],
        compiler_params=pltpu.CompilerParams(vmem_limit_bytes=56 * 1024 * 1024),
        cost_estimate=pl.CostEstimate(
            flops=50 * blocks * rows * width * columns,
            bytes_accessed=2 * (width * columns + blocks * rows * (width + columns)),
            transcendentals=0,
        ),
    )(place, weight, *pieces)


def split_last_kernel(
    place_ref, weight_ref, kept, sent, low_ref, high_ref, keep_ref, send_ref, rows_ref, keeps_ref, sends_ref, arrived
):
    step = pl.program_id(0)
    steps, half, tile = keeps_ref.shape

    @pl.when(step == 0)
    def _():
        rows_ref[:half] = low_ref[...]
        rows_ref[half:] = high_ref[...]

    total = jnp.dot(rows_ref[...], weight_ref[...], preferred_element_type=jnp.float32)
    second = place_ref[2] == 1
    low, high = total[:half], total[half:]
    keeps_ref[step] = jnp.where(second, high, low)
    sends_ref[step] = jnp.where(second, low, high).astype(jnp.bfloat16)

    @pl.when(step == steps - 1)
    def _():
        copies = []
        where = block_of(place_ref, (2, 1))
        for index in range(steps):
            window = pl.ds(index * tile, tile)
            for side, (part_ref, out_ref) in enumerate(((keeps_ref, keep_ref), (sends_ref, send_ref))):
                copies.append(
                    pltpu.make_async_copy(
                        part_ref.at[index], out_ref.at[where, :, window], arrived.at[side, index]
                    )
                )
        for copy in copies:
            copy.start()
        for copy in copies:
            copy.wait()


def split_product_last(place, weight, kept, sent, arrived_rows):
    width, columns = weight.shape
    tile = 512
    half = arrived_rows.shape[0] // 2
    steps = columns // tile
    return pl.pallas_call(
        split_last_kernel,
        grid=(steps,),
        out_shape=[
            jax.ShapeDtypeStruct(kept.shape, jnp.float32),
            jax.ShapeDtypeStruct(sent.shape, jnp.bfloat16),
        ],
        in_specs=[
            pl.BlockSpec(memory_space=pltpu.SMEM),
            pl.BlockSpec((width, tile), lambda i: (0, i)),
            pl.BlockSpec(memory_space=pl.ANY),
            pl.BlockSpec(memory_space=pl.ANY),
            pl.BlockSpec((half, width), lambda i: (0, 0)),
            pl.BlockSpec((half, width), lambda i: (1, 0)),
        ],
        out_specs=[pl.BlockSpec(memory_space=pl.ANY)] * 2,
        scratch_shapes=[
            pltpu.VMEM((2 * half, width), jnp.bfloat16),
            pltpu.VMEM((steps, half, tile), jnp.float32),
            pltpu.VMEM((steps, half, tile), jnp.bfloat16),
            pltpu.SemaphoreType.DMA((2, steps)),
        ],
        input_output_aliases={2: 0, 3: 1},
        compiler_params=pltpu.CompilerParams(vmem_limit_bytes=56 * 1024 * 1024),
        cost_estimate=pl.CostEstimate(
            flops=4 * half * width * columns,
            bytes_accessed=2 * (width * columns + 2 * half * (width + columns)),
            transcendentals=0,
        ),
    )(place, weight, kept, sent, arrived_rows, arrived_rows)


def total_kernel(keep_ref, got_ref, out_ref):
    out_ref[...] = (keep_ref[...] + got_ref[...].astype(jnp.float32)).astype(jnp.bfloat16)


def reduce_shares(keep, send):
    count = lax.axis_size("tp")
    got = lax.ppermute(send, "tp", [(i, i ^ 1) for i in range(count)])
    blocks, rows, columns = keep.shape
    spec = pl.BlockSpec((blocks // 4, rows, columns), lambda i: (i, 0, 0))
    total = pl.pallas_call(
        total_kernel,
        grid=(4,),
        out_shape=jax.ShapeDtypeStruct(keep.shape, jnp.bfloat16),
        in_specs=[spec, spec],
        out_specs=spec,
    )(keep, got)
    groups = [list(range(core, count, 2)) for core in range(2)]
    parts = lax.all_to_all(total, "tp", 0, 0, axis_index_groups=groups, tiled=True)
    return jnp.sum(parts.astype(jnp.float32), axis=0)


def ring(step):
    def move(block):
        count = lax.axis_size("ctx")
        return lax.ppermute(block, "ctx", [(i, (i + 2 * step) % count) for i in range(count)])

    return move


def across(block):
    return lax.ppermute(block, "ctx", [(i, i ^ 1) for i in range(lax.axis_size("ctx"))])


def exchange(block):
    return lax.all_to_all(block, "tp", 0, 0, tiled=True)


def sync(*values):
    return lax.optimization_barrier(values)


def keep(*values):
    return values

def shards(hidden, sign_bits, weight_codes, weight_exps):
    tokens, width = hidden.shape
    columns = weight_codes.shape[1]
    groups = lax.axis_size("tp")
    share = tokens // groups // 2
    matrix = jnp.asarray(np.kron(sylvester(width // 104), paley_matrix()), jnp.bfloat16)
    flips = (1 - 2 * sign_bits).astype(jnp.bfloat16)
    ctx = lax.axis_index("ctx")
    place = jnp.stack([ctx // 2, ctx % 2, lax.axis_index("tp") % 2]).astype(jnp.int32)
    up, down = ring(1), ring(-1)
    rows = tokens // 2
    half, quarter = rows // 2, rows // 4
    cut = hidden.reshape(groups, 2, share, width)
    raw0, raw1 = cut[:, 0] * flips, cut[:, 1] * flips
    got = exchange(raw0)
    weight = decode_weights(weight_codes, weight_exps)
    got, weight, raw1 = sync(got, weight, raw1)
    own0 = exchange(rotate(got, matrix, 0, share)).reshape(rows, width)
    raw1, own0 = sync(raw1, own0)
    got1 = exchange(raw1)
    rotated1 = rotate(got1, matrix, 0, share)
    own0, rotated1, weight = keep(own0, rotated1, weight)

    below0, above0, other0 = up(own0), down(own0), across(own0)
    own1 = exchange(rotated1).reshape(rows, width)
    below0, above0, other0, own1, weight = keep(below0, above0, other0, own1, weight)

    other_below0, other_above0 = up(other0[:half]), down(other0[:half])
    far0 = [up(below0)]
    late0 = across(jnp.concatenate([below0[half:], above0[half:]]))
    other_below0, other_above0, late0, own1, *far0 = keep(
        other_below0, other_above0, late0, own1, *far0
    )

    spec = [(index, 0, rows, index, 0) for index in range(5)]
    spec += [(5, 0, half, 5, 0), (6, 0, half, 6, 0), (7, 0, half, 5, half), (7, half, half, 6, half)]
    last0 = down(other_above0)
    late_far0 = across(far0[0][half:])
    below1, above1, other1 = up(own1), down(own1), across(own1)
    pieces0 = [own0, below0, above0, *far0, other0, other_below0, other_above0, late0]
    part0 = product(place, weight, spec, pieces0)
    below1, above1, other1, late_far0, part0, last0 = keep(
        below1, above1, other1, late_far0, part0, last0
    )

    part0 = product_last(place, weight, part0, last0, late_far0)
    sent0 = exchange(part0.reshape(groups, half, columns))
    other_below1, other_above1 = up(other1), down(other1)
    far1 = [down(above1)]
    other_below1, other_above1, *far1 = keep(other_below1, other_above1, *far1)

    last1 = [up(other_below1)]
    spec1 = [(index, 0, rows, index, 0) for index in range(7)]
    pieces1 = [own1, below1, above1, *far1, other1, other_below1, other_above1]
    kept, sent = split_product(place, weight, spec1, pieces1)
    kept, sent = split_product_last(place, weight, kept, sent, *last1)
    out1 = reduce_shares(kept, sent)
    out0 = jnp.sum(sent0.astype(jnp.float32), axis=0)
    outs = [out.reshape(groups // 2, share, columns) for out in (out0, out1)]
    return jnp.concatenate(outs, axis=1).reshape(rows, columns)


def solution(mesh):
    return jax.shard_map(
        shards,
        mesh=mesh,
        in_specs=(P("ctx", "tp"), P("tp"), P("tp", "ctx"), P("tp", "ctx")),
        out_specs=P("tp", "ctx"),
        check_vma=False,
    )
```

```python
import math

import jax
import jax.numpy as jnp
import numpy as np
from jax import lax
from jax.experimental import pallas as pl
from jax.experimental.pallas import tpu as pltpu
from jax.sharding import PartitionSpec as P


def paley_matrix():
    elements = [(first_part, second_part) for first_part in range(5) for second_part in range(5)]
    squares = set()
    for left_elem in elements:
        if left_elem != (0, 0):
            squares.add(
                (
                    (left_elem[0] * left_elem[0] + 3 * left_elem[1] * left_elem[1]) % 5,
                    2 * left_elem[0] * left_elem[1] % 5,
                )
            )
    jacobs = np.zeros((25, 25))
    for row_index in range(25):
        for col_index in range(25):
            left_elem = elements[row_index]
            right_elem = elements[col_index]
            differ = ((left_elem[0] - right_elem[0]) % 5, (left_elem[1] - right_elem[1]) % 5)
            if differ == (0, 0):
                jacobs[row_index, col_index] = 0.0
            elif differ in squares:
                jacobs[row_index, col_index] = 1.0
            else:
                jacobs[row_index, col_index] = -1.0
    conference = np.zeros((26, 26))
    conference[0, 1:] = 1.0
    conference[1:, 0] = 1.0
    conference[1:, 1:] = jacobs
    result = np.kron(conference, np.array([[1.0, 1.0], [1.0, -1.0]])) + np.kron(
        np.eye(26), np.array([[1.0, -1.0], [-1.0, -1.0]])
    )
    return result


def sylvester(order):
    matrix = np.ones((1, 1))
    while matrix.shape[0] < order:
        matrix = np.kron(np.array([[1.0, 1.0], [1.0, -1.0]]), matrix)
    return matrix


def decode_kernel(codes_ref, exps_ref, out_ref):
    for block in range(exps_ref.shape[0]):
        codes = codes_ref[block * 32 : block * 32 + 32, :]
        scale = jnp.left_shift(1, exps_ref[block : block + 1, :]).astype(jnp.float32) * 2.0 ** (-11)
        scale = jnp.where(codes >= 8, -scale, scale)
        magnitude = jnp.bitwise_and(codes, 7).astype(jnp.float32)
        value = jnp.where(
            magnitude < 4.0,
            magnitude * 0.5,
            jnp.where(magnitude < 6.0, magnitude - 2.0, 2.0 * magnitude - 8.0),
        )
        out_ref[block * 32 : block * 32 + 32, :] = (value * scale).astype(jnp.bfloat16)


def decode_weights(codes, exponents):
    rows, columns = codes.shape
    step = 256
    return pl.pallas_call(
        decode_kernel,
        grid=(rows // step,),
        out_shape=jax.ShapeDtypeStruct(codes.shape, jnp.bfloat16),
        in_specs=[
            pl.BlockSpec((step, columns), lambda i: (i, 0)),
            pl.BlockSpec((step // 32, columns), lambda i: (i, 0)),
        ],
        out_specs=pl.BlockSpec((step, columns), lambda i: (i, 0)),
        compiler_params=pltpu.CompilerParams(vmem_limit_bytes=56 * 1024 * 1024),
        cost_estimate=pl.CostEstimate(
            flops=10 * rows * columns, bytes_accessed=6 * rows * columns, transcendentals=0
        ),
    )(codes, exponents)


def butterfly(parts):
    distance = 1
    while distance < len(parts):
        parts = [
            parts[index] + parts[index + distance]
            if index // distance % 2 == 0
            else parts[index - distance] - parts[index]
            for index in range(len(parts))
        ]
        distance *= 2
    return parts


def rotate_kernel(share, begin, scaling, raw_ref, matrix_ref, out_ref, total_ref, columns_ref, arrived):
    half = matrix_ref.shape[0]
    starts = list(range(0, half, 512))
    copies = []
    for index, start in enumerate(starts):
        window = pl.ds(start, min(512, half - start))
        copies.append(
            pltpu.make_async_copy(
                matrix_ref.at[:, window], columns_ref.at[:, window], arrived.at[index]
            )
        )
    for copy in copies:
        copy.start()
    rows = raw_ref[:, begin : begin + share, :].reshape(-1, 2 * half)
    stacked = jnp.concatenate([rows[:, :half], rows[:, half:]], axis=0)
    for index, start in enumerate(starts):
        width = min(512, half - start)
        copies[index].wait()
        columns = columns_ref[:, start : start + width]
        total_ref[:, :width] = jnp.dot(stacked, columns, preferred_element_type=jnp.float32)
        count = rows.shape[0]
        for lane in range(0, width, 128):
            low, high = (
                [
                    total_ref[base + at : base + at + share, lane : lane + 128]
                    for at in range(0, count, share)
                ]
                for base in (0, count)
            )
            window = slice(start + lane, start + lane + 128)
            other = slice(half + start + lane, half + start + lane + 128)
            for at, (one, two) in enumerate(zip(butterfly(low), butterfly(high))):
                out_ref[at, :, window] = ((one + two) * scaling).astype(jnp.bfloat16)
                out_ref[at, :, other] = ((one - two) * scaling).astype(jnp.bfloat16)


def rotate(raw, matrix, begin, share):
    groups, _, width = raw.shape
    scaling = 1.0 / math.sqrt(groups * width)
    return pl.pallas_call(
        lambda *refs: rotate_kernel(share, begin, scaling, *refs),
        out_shape=jax.ShapeDtypeStruct((groups, share, width), jnp.bfloat16),
        in_specs=[
            pl.BlockSpec(memory_space=pltpu.VMEM),
            pl.BlockSpec(memory_space=pl.ANY),
        ],
        out_specs=pl.BlockSpec(memory_space=pltpu.VMEM),
        scratch_shapes=[
            pltpu.VMEM((2 * groups * share, 512), jnp.float32),
            pltpu.VMEM(matrix.shape, jnp.bfloat16),
            pltpu.SemaphoreType.DMA((-(-matrix.shape[0] // 512),)),
        ],
        compiler_params=pltpu.CompilerParams(vmem_limit_bytes=56 * 1024 * 1024),
        cost_estimate=pl.CostEstimate(
            flops=2 * groups * share * width * (width // 2),
            bytes_accessed=width * width // 2 + 4 * groups * share * width,
            transcendentals=0,
        ),
    )(raw, matrix)


def block_of(place_ref, shift):
    return lax.rem(place_ref[0] + shift[0], 4) * 2 + lax.rem(place_ref[1] + shift[1], 2)


def product_kernel(spec, shifts, place_ref, weight_ref, *refs):
    pieces = refs[:-3]
    out_ref, rows_ref, arrived = refs[-3:]
    blocks, n_rows, width = rows_ref.shape

    @pl.when(pl.program_id(0) == 0)
    def _():
        copies = []
        for index, (source, begin, count, block, start) in enumerate(spec):
            window = rows_ref.at[block, pl.ds(start, count)]
            block_rows = pieces[source].at[pl.ds(begin, count)]
            copies.append(pltpu.make_async_copy(block_rows, window, arrived.at[index]))
        for copy in copies:
            copy.start()
        for copy in copies:
            copy.wait()

    total = (
        jnp.dot(
            rows_ref[...].reshape(blocks * n_rows, width),
            weight_ref[...],
            preferred_element_type=jnp.float32,
        )
        .reshape(blocks, n_rows, weight_ref.shape[1])
        .astype(jnp.bfloat16)
    )
    for block, shift in enumerate(shifts):
        out_ref[block_of(place_ref, shift)] = total[block]


def product(place, weight, spec, pieces):
    width, columns = weight.shape
    tile = 256
    blocks = 7
    rows = sum(piece.shape[0] for piece in pieces) // blocks
    shifts = [(0, 0), (3, 0), (1, 0), (2, 0), (0, 1), (3, 1), (1, 1)]
    return pl.pallas_call(
        lambda *refs: product_kernel(spec, shifts, *refs),
        grid=(columns // tile,),
        out_shape=jax.ShapeDtypeStruct((blocks + 1, rows, columns), jnp.bfloat16),
        in_specs=[
            pl.BlockSpec(memory_space=pltpu.SMEM),
            pl.BlockSpec((width, tile), lambda i: (0, i)),
        ]
        + [pl.BlockSpec(memory_space=pl.ANY)] * len(pieces),
        out_specs=pl.BlockSpec((blocks + 1, rows, tile), lambda i: (0, 0, i)),
        scratch_shapes=[
            pltpu.VMEM((blocks, rows, width), jnp.bfloat16),
            pltpu.SemaphoreType.DMA((len(spec),)),
        ],
        compiler_params=pltpu.CompilerParams(vmem_limit_bytes=56 * 1024 * 1024),
        cost_estimate=pl.CostEstimate(
            flops=50 * blocks * rows * width * columns,
            bytes_accessed=2 * (width * columns + blocks * rows * (width + columns)),
            transcendentals=0,
        ),
    )(place, weight, *pieces)


def last_kernel(place_ref, weight_ref, before_ref, low_ref, high_ref, out_ref, rows_ref, total_ref, arrived):
    step = pl.program_id(0)
    half = low_ref.shape[0]
    tile = weight_ref.shape[1]

    @pl.when(step == 0)
    def _():
        rows_ref[:half] = low_ref[...]
        rows_ref[half:] = high_ref[...]

    total_ref[step] = jnp.dot(
        rows_ref[...], weight_ref[...], preferred_element_type=jnp.float32
    ).astype(jnp.bfloat16)

    @pl.when(step == total_ref.shape[0] - 1)
    def _():
        copies = []
        for index in range(total_ref.shape[0]):
            window = out_ref.at[block_of(place_ref, (2, 1)), :, pl.ds(index * tile, tile)]
            copies.append(pltpu.make_async_copy(total_ref.at[index], window, arrived.at[index]))
        for copy in copies:
            copy.start()
        for copy in copies:
            copy.wait()


def product_last(place, weight, before, low, high):
    width, columns = weight.shape
    tile = 512
    rows = 2 * low.shape[0]
    return pl.pallas_call(
        last_kernel,
        grid=(columns // tile,),
        out_shape=jax.ShapeDtypeStruct(before.shape, jnp.bfloat16),
        in_specs=[
            pl.BlockSpec(memory_space=pltpu.SMEM),
            pl.BlockSpec((width, tile), lambda i: (0, i)),
            pl.BlockSpec(memory_space=pl.ANY),
            pl.BlockSpec(low.shape, lambda i: (0, 0)),
            pl.BlockSpec(high.shape, lambda i: (0, 0)),
        ],
        out_specs=pl.BlockSpec(memory_space=pl.ANY),
        scratch_shapes=[
            pltpu.VMEM((rows, width), jnp.bfloat16),
            pltpu.VMEM((columns // tile, rows, tile), jnp.bfloat16),
            pltpu.SemaphoreType.DMA((columns // tile,)),
        ],
        input_output_aliases={2: 0},
        compiler_params=pltpu.CompilerParams(vmem_limit_bytes=56 * 1024 * 1024),
        cost_estimate=pl.CostEstimate(
            flops=2 * rows * width * columns,
            bytes_accessed=2 * (width * columns + rows * (width + columns)),
            transcendentals=0,
        ),
    )(place, weight, before, low, high)


def split_product_kernel(spec, shifts, place_ref, weight_ref, *refs):
    pieces = refs[:-4]
    keep_ref, send_ref, rows_ref, arrived = refs[-4:]
    blocks, n_rows, width = rows_ref.shape

    @pl.when(pl.program_id(0) == 0)
    def _():
        copies = []
        for index, (source, begin, count, block, start) in enumerate(spec):
            window = rows_ref.at[block, pl.ds(start, count)]
            block_rows = pieces[source].at[pl.ds(begin, count)]
            copies.append(pltpu.make_async_copy(block_rows, window, arrived.at[index]))
        for copy in copies:
            copy.start()
        for copy in copies:
            copy.wait()

    total = jnp.dot(
        rows_ref[...].reshape(blocks * n_rows, width),
        weight_ref[...],
        preferred_element_type=jnp.float32,
    ).reshape(blocks, 2, n_rows // 2, weight_ref.shape[1])
    second = place_ref[2] == 1
    for block, shift in enumerate(shifts):
        where = block_of(place_ref, shift)
        low, high = total[block, 0], total[block, 1]
        keep_ref[where] = jnp.where(second, high, low)
        send_ref[where] = jnp.where(second, low, high).astype(jnp.bfloat16)


def split_product(place, weight, spec, pieces):
    width, columns = weight.shape
    tile = 256
    blocks = 7
    rows = sum(count for _, _, count, _, _ in spec) // blocks
    shifts = [(0, 0), (3, 0), (1, 0), (2, 0), (0, 1), (3, 1), (1, 1)]
    shape = (blocks + 1, rows // 2, columns)
    block = pl.BlockSpec((blocks + 1, rows // 2, tile), lambda i: (0, 0, i))
    return pl.pallas_call(
        lambda *refs: split_product_kernel(spec, shifts, *refs),
        grid=(columns // tile,),
        out_shape=[
            jax.ShapeDtypeStruct(shape, jnp.float32),
            jax.ShapeDtypeStruct(shape, jnp.bfloat16),
        ],
        in_specs=[
            pl.BlockSpec(memory_space=pltpu.SMEM),
            pl.BlockSpec((width, tile), lambda i: (0, i)),
        ]
        + [pl.BlockSpec(memory_space=pl.ANY)] * len(pieces),
        out_specs=[block, block],
        scratch_shapes=[
            pltpu.VMEM((blocks, rows, width), jnp.bfloat16),
            pltpu.SemaphoreType.DMA((len(spec),)),
        ],
        compiler_params=pltpu.CompilerParams(vmem_limit_bytes=56 * 1024 * 1024),
        cost_estimate=pl.CostEstimate(
            flops=50 * blocks * rows * width * columns,
            bytes_accessed=2 * (width * columns + blocks * rows * (width + columns)),
            transcendentals=0,
        ),
    )(place, weight, *pieces)


def split_last_kernel(
    place_ref, weight_ref, kept, sent, low_ref, high_ref, keep_ref, send_ref, rows_ref, keeps_ref, sends_ref, arrived
):
    step = pl.program_id(0)
    steps, half, tile = keeps_ref.shape

    @pl.when(step == 0)
    def _():
        rows_ref[:half] = low_ref[...]
        rows_ref[half:] = high_ref[...]

    total = jnp.dot(rows_ref[...], weight_ref[...], preferred_element_type=jnp.float32)
    second = place_ref[2] == 1
    low, high = total[:half], total[half:]
    keeps_ref[step] = jnp.where(second, high, low)
    sends_ref[step] = jnp.where(second, low, high).astype(jnp.bfloat16)

    @pl.when(step == steps - 1)
    def _():
        copies = []
        where = block_of(place_ref, (2, 1))
        for index in range(steps):
            window = pl.ds(index * tile, tile)
            for side, (part_ref, out_ref) in enumerate(((keeps_ref, keep_ref), (sends_ref, send_ref))):
                copies.append(
                    pltpu.make_async_copy(
                        part_ref.at[index], out_ref.at[where, :, window], arrived.at[side, index]
                    )
                )
        for copy in copies:
            copy.start()
        for copy in copies:
            copy.wait()


def split_product_last(place, weight, kept, sent, arrived_rows):
    width, columns = weight.shape
    tile = 512
    half = arrived_rows.shape[0] // 2
    steps = columns // tile
    return pl.pallas_call(
        split_last_kernel,
        grid=(steps,),
        out_shape=[
            jax.ShapeDtypeStruct(kept.shape, jnp.float32),
            jax.ShapeDtypeStruct(sent.shape, jnp.bfloat16),
        ],
        in_specs=[
            pl.BlockSpec(memory_space=pltpu.SMEM),
            pl.BlockSpec((width, tile), lambda i: (0, i)),
            pl.BlockSpec(memory_space=pl.ANY),
            pl.BlockSpec(memory_space=pl.ANY),
            pl.BlockSpec((half, width), lambda i: (0, 0)),
            pl.BlockSpec((half, width), lambda i: (1, 0)),
        ],
        out_specs=[pl.BlockSpec(memory_space=pl.ANY)] * 2,
        scratch_shapes=[
            pltpu.VMEM((2 * half, width), jnp.bfloat16),
            pltpu.VMEM((steps, half, tile), jnp.float32),
            pltpu.VMEM((steps, half, tile), jnp.bfloat16),
            pltpu.SemaphoreType.DMA((2, steps)),
        ],
        input_output_aliases={2: 0, 3: 1},
        compiler_params=pltpu.CompilerParams(vmem_limit_bytes=56 * 1024 * 1024),
        cost_estimate=pl.CostEstimate(
            flops=4 * half * width * columns,
            bytes_accessed=2 * (width * columns + 2 * half * (width + columns)),
            transcendentals=0,
        ),
    )(place, weight, kept, sent, arrived_rows, arrived_rows)


def reduce_shares(keep, send):
    count = lax.axis_size("tp")
    got = lax.ppermute(send, "tp", [(i, i ^ 1) for i in range(count)])
    total = (keep + got.astype(jnp.float32)).astype(jnp.bfloat16)
    groups = [list(range(core, count, 2)) for core in range(2)]
    parts = lax.all_to_all(total, "tp", 0, 0, axis_index_groups=groups, tiled=True)
    return jnp.sum(parts.astype(jnp.float32), axis=0)


def ring(step):
    def move(block):
        count = lax.axis_size("ctx")
        return lax.ppermute(block, "ctx", [(i, (i + 2 * step) % count) for i in range(count)])

    return move


def across(block):
    return lax.ppermute(block, "ctx", [(i, i ^ 1) for i in range(lax.axis_size("ctx"))])


def exchange(block):
    return lax.all_to_all(block, "tp", 0, 0, tiled=True)


def sync(*values):
    return lax.optimization_barrier(values)


def keep(*values):
    return values

def shards(hidden, sign_bits, weight_codes, weight_exps):
    tokens, width = hidden.shape
    columns = weight_codes.shape[1]
    groups = lax.axis_size("tp")
    share = tokens // groups // 2
    matrix = jnp.asarray(np.kron(sylvester(width // 104), paley_matrix()), jnp.bfloat16)
    flips = (1 - 2 * sign_bits).astype(jnp.bfloat16)
    ctx = lax.axis_index("ctx")
    place = jnp.stack([ctx // 2, ctx % 2, lax.axis_index("tp") % 2]).astype(jnp.int32)
    up, down = ring(1), ring(-1)
    rows = tokens // 2
    half, quarter = rows // 2, rows // 4
    cut = hidden.reshape(groups, 2, share, width)
    raw0, raw1 = cut[:, 0] * flips, cut[:, 1] * flips
    got = exchange(raw0)
    weight = decode_weights(weight_codes, weight_exps)
    got, weight, raw1 = sync(got, weight, raw1)
    own0 = exchange(rotate(got, matrix, 0, share)).reshape(rows, width)
    raw1, own0 = sync(raw1, own0)
    got1 = exchange(raw1)
    rotated1 = rotate(got1, matrix, 0, share)
    own0, rotated1, weight = keep(own0, rotated1, weight)

    below0, above0, other0 = up(own0), down(own0), across(own0)
    own1 = exchange(rotated1).reshape(rows, width)
    below0, above0, other0, own1, weight = keep(below0, above0, other0, own1, weight)

    other_below0, other_above0 = up(other0[:half]), down(other0[:half])
    far0 = [up(below0)]
    late0 = across(jnp.concatenate([below0[half:], above0[half:]]))
    other_below0, other_above0, late0, own1, *far0 = keep(
        other_below0, other_above0, late0, own1, *far0
    )

    spec = [(index, 0, rows, index, 0) for index in range(5)]
    spec += [(5, 0, half, 5, 0), (6, 0, half, 6, 0), (7, 0, half, 5, half), (7, half, half, 6, half)]
    last0 = down(other_above0)
    late_far0 = across(far0[0][half:])
    below1, above1, other1 = up(own1), down(own1), across(own1)
    pieces0 = [own0, below0, above0, *far0, other0, other_below0, other_above0, late0]
    part0 = product(place, weight, spec, pieces0)
    below1, above1, other1, late_far0, part0, last0 = keep(
        below1, above1, other1, late_far0, part0, last0
    )

    part0 = product_last(place, weight, part0, last0, late_far0)
    sent0 = exchange(part0.reshape(groups, half, columns))
    other_below1, other_above1 = up(other1), down(other1)
    far1 = [down(above1)]
    other_below1, other_above1, *far1 = keep(other_below1, other_above1, *far1)

    last1 = [up(other_below1)]
    spec1 = [(index, 0, rows, index, 0) for index in range(7)]
    pieces1 = [own1, below1, above1, *far1, other1, other_below1, other_above1]
    kept, sent = split_product(place, weight, spec1, pieces1)
    kept, sent = split_product_last(place, weight, kept, sent, *last1)
    out1 = reduce_shares(kept, sent)
    out0 = jnp.sum(sent0.astype(jnp.float32), axis=0)
    outs = [out.reshape(groups // 2, share, columns) for out in (out0, out1)]
    return jnp.concatenate(outs, axis=1).reshape(rows, columns)


def solution(mesh):
    return jax.shard_map(
        shards,
        mesh=mesh,
        in_specs=(P("ctx", "tp"), P("tp"), P("tp", "ctx"), P("tp", "ctx")),
        out_specs=P("tp", "ctx"),
        check_vma=False,
    )
```

```python
import math

import jax
import jax.numpy as jnp
import numpy as np
from jax import lax
from jax.experimental import pallas as pl
from jax.experimental.pallas import tpu as pltpu
from jax.sharding import PartitionSpec as P


def paley_matrix():
    elements = [(first_part, second_part) for first_part in range(5) for second_part in range(5)]
    squares = set()
    for left_elem in elements:
        if left_elem != (0, 0):
            squares.add(
                (
                    (left_elem[0] * left_elem[0] + 3 * left_elem[1] * left_elem[1]) % 5,
                    2 * left_elem[0] * left_elem[1] % 5,
                )
            )
    jacobs = np.zeros((25, 25))
    for row_index in range(25):
        for col_index in range(25):
            left_elem = elements[row_index]
            right_elem = elements[col_index]
            differ = ((left_elem[0] - right_elem[0]) % 5, (left_elem[1] - right_elem[1]) % 5)
            if differ == (0, 0):
                jacobs[row_index, col_index] = 0.0
            elif differ in squares:
                jacobs[row_index, col_index] = 1.0
            else:
                jacobs[row_index, col_index] = -1.0
    conference = np.zeros((26, 26))
    conference[0, 1:] = 1.0
    conference[1:, 0] = 1.0
    conference[1:, 1:] = jacobs
    result = np.kron(conference, np.array([[1.0, 1.0], [1.0, -1.0]])) + np.kron(
        np.eye(26), np.array([[1.0, -1.0], [-1.0, -1.0]])
    )
    return result


def sylvester(order):
    matrix = np.ones((1, 1))
    while matrix.shape[0] < order:
        matrix = np.kron(np.array([[1.0, 1.0], [1.0, -1.0]]), matrix)
    return matrix


def decode_kernel(codes_ref, exps_ref, out_ref):
    for block in range(exps_ref.shape[0]):
        codes = codes_ref[block * 32 : block * 32 + 32, :]
        scale = jnp.left_shift(1, exps_ref[block : block + 1, :]).astype(jnp.float32) * 2.0 ** (-11)
        scale = jnp.where(codes >= 8, -scale, scale)
        magnitude = jnp.bitwise_and(codes, 7).astype(jnp.float32)
        value = jnp.where(
            magnitude < 4.0,
            magnitude * 0.5,
            jnp.where(magnitude < 6.0, magnitude - 2.0, 2.0 * magnitude - 8.0),
        )
        out_ref[block * 32 : block * 32 + 32, :] = (value * scale).astype(jnp.bfloat16)


def decode_weights(codes, exponents):
    rows, columns = codes.shape
    step = 256
    return pl.pallas_call(
        decode_kernel,
        grid=(rows // step,),
        out_shape=jax.ShapeDtypeStruct(codes.shape, jnp.bfloat16),
        in_specs=[
            pl.BlockSpec((step, columns), lambda i: (i, 0)),
            pl.BlockSpec((step // 32, columns), lambda i: (i, 0)),
        ],
        out_specs=pl.BlockSpec((step, columns), lambda i: (i, 0)),
        compiler_params=pltpu.CompilerParams(vmem_limit_bytes=56 * 1024 * 1024),
        cost_estimate=pl.CostEstimate(
            flops=10 * rows * columns, bytes_accessed=6 * rows * columns, transcendentals=0
        ),
    )(codes, exponents)


def butterfly(parts):
    distance = 1
    while distance < len(parts):
        parts = [
            parts[index] + parts[index + distance]
            if index // distance % 2 == 0
            else parts[index - distance] - parts[index]
            for index in range(len(parts))
        ]
        distance *= 2
    return parts


def rotate_kernel(share, begin, scaling, raw_ref, matrix_ref, out_ref, total_ref, columns_ref, arrived):
    half = matrix_ref.shape[0]
    starts = list(range(0, half, 512))
    copies = []
    for index, start in enumerate(starts):
        window = pl.ds(start, min(512, half - start))
        copies.append(
            pltpu.make_async_copy(
                matrix_ref.at[:, window], columns_ref.at[:, window], arrived.at[index]
            )
        )
    for copy in copies:
        copy.start()
    rows = raw_ref[:, begin : begin + share, :].reshape(-1, 2 * half)
    stacked = jnp.concatenate([rows[:, :half], rows[:, half:]], axis=0)
    for index, start in enumerate(starts):
        width = min(512, half - start)
        copies[index].wait()
        columns = columns_ref[:, start : start + width]
        total_ref[:, :width] = jnp.dot(stacked, columns, preferred_element_type=jnp.float32)
        count = rows.shape[0]
        for lane in range(0, width, 128):
            low, high = (
                [
                    total_ref[base + at : base + at + share, lane : lane + 128]
                    for at in range(0, count, share)
                ]
                for base in (0, count)
            )
            window = slice(start + lane, start + lane + 128)
            other = slice(half + start + lane, half + start + lane + 128)
            for at, (one, two) in enumerate(zip(butterfly(low), butterfly(high))):
                out_ref[at, :, window] = ((one + two) * scaling).astype(jnp.bfloat16)
                out_ref[at, :, other] = ((one - two) * scaling).astype(jnp.bfloat16)


def rotate(raw, matrix, begin, share):
    groups, _, width = raw.shape
    scaling = 1.0 / math.sqrt(groups * width)
    return pl.pallas_call(
        lambda *refs: rotate_kernel(share, begin, scaling, *refs),
        out_shape=jax.ShapeDtypeStruct((groups, share, width), jnp.bfloat16),
        in_specs=[
            pl.BlockSpec(memory_space=pltpu.VMEM),
            pl.BlockSpec(memory_space=pl.ANY),
        ],
        out_specs=pl.BlockSpec(memory_space=pltpu.VMEM),
        scratch_shapes=[
            pltpu.VMEM((2 * groups * share, 512), jnp.float32),
            pltpu.VMEM(matrix.shape, jnp.bfloat16),
            pltpu.SemaphoreType.DMA((-(-matrix.shape[0] // 512),)),
        ],
        compiler_params=pltpu.CompilerParams(vmem_limit_bytes=56 * 1024 * 1024),
        cost_estimate=pl.CostEstimate(
            flops=2 * groups * share * width * (width // 2),
            bytes_accessed=width * width // 2 + 4 * groups * share * width,
            transcendentals=0,
        ),
    )(raw, matrix)


def block_of(place_ref, shift):
    return lax.rem(place_ref[0] + shift[0], 4) * 2 + lax.rem(place_ref[1] + shift[1], 2)


def product_kernel(spec, shifts, place_ref, weight_ref, *refs):
    pieces = refs[:-3]
    out_ref, rows_ref, arrived = refs[-3:]
    blocks, n_rows, width = rows_ref.shape

    @pl.when(pl.program_id(0) == 0)
    def _():
        copies = []
        for index, (source, begin, count, block, start) in enumerate(spec):
            window = rows_ref.at[block, pl.ds(start, count)]
            block_rows = pieces[source].at[pl.ds(begin, count)]
            copies.append(pltpu.make_async_copy(block_rows, window, arrived.at[index]))
        for copy in copies:
            copy.start()
        for copy in copies:
            copy.wait()

    total = (
        jnp.dot(
            rows_ref[...].reshape(blocks * n_rows, width),
            weight_ref[...],
            preferred_element_type=jnp.float32,
        )
        .reshape(blocks, n_rows, weight_ref.shape[1])
        .astype(jnp.bfloat16)
    )
    for block, shift in enumerate(shifts):
        out_ref[block_of(place_ref, shift)] = total[block]


def product(place, weight, spec, pieces):
    width, columns = weight.shape
    tile = 256
    blocks = 7
    rows = sum(piece.shape[0] for piece in pieces) // blocks
    shifts = [(0, 0), (3, 0), (1, 0), (2, 0), (0, 1), (3, 1), (1, 1)]
    return pl.pallas_call(
        lambda *refs: product_kernel(spec, shifts, *refs),
        grid=(columns // tile,),
        out_shape=jax.ShapeDtypeStruct((blocks + 1, rows, columns), jnp.bfloat16),
        in_specs=[
            pl.BlockSpec(memory_space=pltpu.SMEM),
            pl.BlockSpec((width, tile), lambda i: (0, i)),
        ]
        + [pl.BlockSpec(memory_space=pl.ANY)] * len(pieces),
        out_specs=pl.BlockSpec((blocks + 1, rows, tile), lambda i: (0, 0, i)),
        scratch_shapes=[
            pltpu.VMEM((blocks, rows, width), jnp.bfloat16),
            pltpu.SemaphoreType.DMA((len(spec),)),
        ],
        compiler_params=pltpu.CompilerParams(vmem_limit_bytes=56 * 1024 * 1024),
        cost_estimate=pl.CostEstimate(
            flops=50 * blocks * rows * width * columns,
            bytes_accessed=2 * (width * columns + blocks * rows * (width + columns)),
            transcendentals=0,
        ),
    )(place, weight, *pieces)


def last_kernel(place_ref, weight_ref, before_ref, low_ref, high_ref, out_ref, rows_ref, total_ref, arrived):
    step = pl.program_id(0)
    half = low_ref.shape[0]
    tile = weight_ref.shape[1]

    @pl.when(step == 0)
    def _():
        rows_ref[:half] = low_ref[...]
        rows_ref[half:] = high_ref[...]

    total_ref[step] = jnp.dot(
        rows_ref[...], weight_ref[...], preferred_element_type=jnp.float32
    ).astype(jnp.bfloat16)

    @pl.when(step == total_ref.shape[0] - 1)
    def _():
        copies = []
        for index in range(total_ref.shape[0]):
            window = out_ref.at[block_of(place_ref, (2, 1)), :, pl.ds(index * tile, tile)]
            copies.append(pltpu.make_async_copy(total_ref.at[index], window, arrived.at[index]))
        for copy in copies:
            copy.start()
        for copy in copies:
            copy.wait()


def product_last(place, weight, before, low, high):
    width, columns = weight.shape
    tile = 512
    rows = 2 * low.shape[0]
    return pl.pallas_call(
        last_kernel,
        grid=(columns // tile,),
        out_shape=jax.ShapeDtypeStruct(before.shape, jnp.bfloat16),
        in_specs=[
            pl.BlockSpec(memory_space=pltpu.SMEM),
            pl.BlockSpec((width, tile), lambda i: (0, i)),
            pl.BlockSpec(memory_space=pl.ANY),
            pl.BlockSpec(low.shape, lambda i: (0, 0)),
            pl.BlockSpec(high.shape, lambda i: (0, 0)),
        ],
        out_specs=pl.BlockSpec(memory_space=pl.ANY),
        scratch_shapes=[
            pltpu.VMEM((rows, width), jnp.bfloat16),
            pltpu.VMEM((columns // tile, rows, tile), jnp.bfloat16),
            pltpu.SemaphoreType.DMA((columns // tile,)),
        ],
        input_output_aliases={2: 0},
        compiler_params=pltpu.CompilerParams(vmem_limit_bytes=56 * 1024 * 1024),
        cost_estimate=pl.CostEstimate(
            flops=2 * rows * width * columns,
            bytes_accessed=2 * (width * columns + rows * (width + columns)),
            transcendentals=0,
        ),
    )(place, weight, before, low, high)


def split_product_kernel(spec, shifts, place_ref, weight_ref, *refs):
    pieces = refs[:-4]
    keep_ref, send_ref, rows_ref, arrived = refs[-4:]
    blocks, n_rows, width = rows_ref.shape

    @pl.when(pl.program_id(0) == 0)
    def _():
        copies = []
        for index, (source, begin, count, block, start) in enumerate(spec):
            window = rows_ref.at[block, pl.ds(start, count)]
            block_rows = pieces[source].at[pl.ds(begin, count)]
            copies.append(pltpu.make_async_copy(block_rows, window, arrived.at[index]))
        for copy in copies:
            copy.start()
        for copy in copies:
            copy.wait()

    total = jnp.dot(
        rows_ref[...].reshape(blocks * n_rows, width),
        weight_ref[...],
        preferred_element_type=jnp.float32,
    ).reshape(blocks, 2, n_rows // 2, weight_ref.shape[1])
    second = place_ref[2] == 1
    for block, shift in enumerate(shifts):
        where = block_of(place_ref, shift)
        low, high = total[block, 0], total[block, 1]
        keep_ref[where] = jnp.where(second, high, low)
        send_ref[where] = jnp.where(second, low, high).astype(jnp.bfloat16)


def split_product(place, weight, spec, pieces):
    width, columns = weight.shape
    tile = 256
    blocks = 7
    rows = sum(count for _, _, count, _, _ in spec) // blocks
    shifts = [(0, 0), (3, 0), (1, 0), (2, 0), (0, 1), (3, 1), (1, 1)]
    shape = (blocks + 1, rows // 2, columns)
    block = pl.BlockSpec((blocks + 1, rows // 2, tile), lambda i: (0, 0, i))
    return pl.pallas_call(
        lambda *refs: split_product_kernel(spec, shifts, *refs),
        grid=(columns // tile,),
        out_shape=[
            jax.ShapeDtypeStruct(shape, jnp.float32),
            jax.ShapeDtypeStruct(shape, jnp.bfloat16),
        ],
        in_specs=[
            pl.BlockSpec(memory_space=pltpu.SMEM),
            pl.BlockSpec((width, tile), lambda i: (0, i)),
        ]
        + [pl.BlockSpec(memory_space=pl.ANY)] * len(pieces),
        out_specs=[block, block],
        scratch_shapes=[
            pltpu.VMEM((blocks, rows, width), jnp.bfloat16),
            pltpu.SemaphoreType.DMA((len(spec),)),
        ],
        compiler_params=pltpu.CompilerParams(vmem_limit_bytes=56 * 1024 * 1024),
        cost_estimate=pl.CostEstimate(
            flops=50 * blocks * rows * width * columns,
            bytes_accessed=2 * (width * columns + blocks * rows * (width + columns)),
            transcendentals=0,
        ),
    )(place, weight, *pieces)


def split_last_kernel(
    place_ref, weight_ref, kept, sent, low_ref, high_ref, keep_ref, send_ref, rows_ref, keeps_ref, sends_ref, arrived
):
    step = pl.program_id(0)
    steps, half, tile = keeps_ref.shape

    @pl.when(step == 0)
    def _():
        rows_ref[:half] = low_ref[...]
        rows_ref[half:] = high_ref[...]

    total = jnp.dot(rows_ref[...], weight_ref[...], preferred_element_type=jnp.float32)
    second = place_ref[2] == 1
    low, high = total[:half], total[half:]
    keeps_ref[step] = jnp.where(second, high, low)
    sends_ref[step] = jnp.where(second, low, high).astype(jnp.bfloat16)

    @pl.when(step == steps - 1)
    def _():
        copies = []
        where = block_of(place_ref, (2, 1))
        for index in range(steps):
            window = pl.ds(index * tile, tile)
            for side, (part_ref, out_ref) in enumerate(((keeps_ref, keep_ref), (sends_ref, send_ref))):
                copies.append(
                    pltpu.make_async_copy(
                        part_ref.at[index], out_ref.at[where, :, window], arrived.at[side, index]
                    )
                )
        for copy in copies:
            copy.start()
        for copy in copies:
            copy.wait()


def split_product_last(place, weight, kept, sent, arrived_rows):
    width, columns = weight.shape
    tile = 512
    half = arrived_rows.shape[0] // 2
    steps = columns // tile
    return pl.pallas_call(
        split_last_kernel,
        grid=(steps,),
        out_shape=[
            jax.ShapeDtypeStruct(kept.shape, jnp.float32),
            jax.ShapeDtypeStruct(sent.shape, jnp.bfloat16),
        ],
        in_specs=[
            pl.BlockSpec(memory_space=pltpu.SMEM),
            pl.BlockSpec((width, tile), lambda i: (0, i)),
            pl.BlockSpec(memory_space=pl.ANY),
            pl.BlockSpec(memory_space=pl.ANY),
            pl.BlockSpec((half, width), lambda i: (0, 0)),
            pl.BlockSpec((half, width), lambda i: (1, 0)),
        ],
        out_specs=[pl.BlockSpec(memory_space=pl.ANY)] * 2,
        scratch_shapes=[
            pltpu.VMEM((2 * half, width), jnp.bfloat16),
            pltpu.VMEM((steps, half, tile), jnp.float32),
            pltpu.VMEM((steps, half, tile), jnp.bfloat16),
            pltpu.SemaphoreType.DMA((2, steps)),
        ],
        input_output_aliases={2: 0, 3: 1},
        compiler_params=pltpu.CompilerParams(vmem_limit_bytes=56 * 1024 * 1024),
        cost_estimate=pl.CostEstimate(
            flops=4 * half * width * columns,
            bytes_accessed=2 * (width * columns + 2 * half * (width + columns)),
            transcendentals=0,
        ),
    )(place, weight, kept, sent, arrived_rows, arrived_rows)


def reduce_shares(keep, send):
    count = lax.axis_size("tp")
    got = lax.ppermute(send, "tp", [(i, i ^ 1) for i in range(count)])
    total = (keep + got.astype(jnp.float32)).astype(jnp.bfloat16)
    groups = [list(range(core, count, 2)) for core in range(2)]
    parts = lax.all_to_all(total, "tp", 0, 0, axis_index_groups=groups, tiled=True)
    return jnp.sum(parts.astype(jnp.float32), axis=0)


def ring(step):
    def move(block):
        count = lax.axis_size("ctx")
        return lax.ppermute(block, "ctx", [(i, (i + 2 * step) % count) for i in range(count)])

    return move


def across(block):
    return lax.ppermute(block, "ctx", [(i, i ^ 1) for i in range(lax.axis_size("ctx"))])


def exchange(block):
    return lax.all_to_all(block, "tp", 0, 0, tiled=True)


def sync(*values):
    return lax.optimization_barrier(values)


def keep(*values):
    return values

def shards(hidden, sign_bits, weight_codes, weight_exps):
    tokens, width = hidden.shape
    columns = weight_codes.shape[1]
    groups = lax.axis_size("tp")
    share = tokens // groups // 2
    matrix = jnp.asarray(np.kron(sylvester(width // 104), paley_matrix()), jnp.bfloat16)
    flips = (1 - 2 * sign_bits).astype(jnp.bfloat16)
    ctx = lax.axis_index("ctx")
    place = jnp.stack([ctx // 2, ctx % 2, lax.axis_index("tp") % 2]).astype(jnp.int32)
    up, down = ring(1), ring(-1)
    rows = tokens // 2
    half, quarter = rows // 2, rows // 4
    cut = hidden.reshape(groups, 2, share, width)
    raw0, raw1 = cut[:, 0] * flips, cut[:, 1] * flips
    got = exchange(raw0)
    weight = decode_weights(weight_codes, weight_exps)
    got, weight, raw1 = sync(got, weight, raw1)
    own0 = exchange(rotate(got, matrix, 0, share)).reshape(rows, width)
    raw1, own0 = sync(raw1, own0)
    got1 = exchange(raw1)
    rotated1 = rotate(got1, matrix, 0, share)
    own0, rotated1, weight = keep(own0, rotated1, weight)

    below0, above0, other0 = up(own0), down(own0), across(own0)
    own1 = exchange(rotated1).reshape(rows, width)
    below0, above0, other0, own1, weight = keep(below0, above0, other0, own1, weight)

    other_below0, other_above0 = up(other0[:half]), down(other0[:half])
    far0 = [up(below0)]
    late0 = across(jnp.concatenate([below0[half:], above0[half:]]))
    other_below0, other_above0, late0, own1, *far0 = keep(
        other_below0, other_above0, late0, own1, *far0
    )

    spec = [(index, 0, rows, index, 0) for index in range(5)]
    spec += [(5, 0, half, 5, 0), (6, 0, half, 6, 0), (7, 0, half, 5, half), (7, half, half, 6, half)]
    last0 = down(other_above0)
    late_far0 = across(far0[0][half:])
    below1, above1, other1 = up(own1), down(own1), across(own1)
    pieces0 = [own0, below0, above0, *far0, other0, other_below0, other_above0, late0]
    part0 = product(place, weight, spec, pieces0)
    below1, above1, other1, late_far0, part0, last0 = keep(
        below1, above1, other1, late_far0, part0, last0
    )

    part0 = product_last(place, weight, part0, last0, late_far0)
    sent0 = exchange(part0.reshape(groups, half, columns))
    other_below1, other_above1 = up(other1), down(other1)
    far1 = [up(below1)]
    other_below1, other_above1, *far1 = keep(other_below1, other_above1, *far1)

    last1 = [down(other_above1)]
    spec1 = [(index, 0, rows, index, 0) for index in range(7)]
    pieces1 = [own1, below1, above1, *far1, other1, other_below1, other_above1]
    kept, sent = split_product(place, weight, spec1, pieces1)
    kept, sent = split_product_last(place, weight, kept, sent, *last1)
    out1 = reduce_shares(kept, sent)
    out0 = jnp.sum(sent0.astype(jnp.float32), axis=0)
    outs = [out.reshape(groups // 2, share, columns) for out in (out0, out1)]
    return jnp.concatenate(outs, axis=1).reshape(rows, columns)


def solution(mesh):
    return jax.shard_map(
        shards,
        mesh=mesh,
        in_specs=(P("ctx", "tp"), P("tp"), P("tp", "ctx"), P("tp", "ctx")),
        out_specs=P("tp", "ctx"),
        check_vma=False,
    )
```
